256 devices in a mesh: sector: 32 (over z, y), term: 8 (over x, core).
Axes of the slice: x: 4, y: 4, z: 8, core: 2. Of those that a mesh axis runs over, the one named last changes fastest.
Arguments:
- wavefunction: bfloat16 [2, 128, 256, 256], P(None, 'sector'), may hold values from -6 to 6
- left_ops: bfloat16 [64, 128, 256, 256], P('term', 'sector'), may hold values from -0.375 to 0.375
- right_ops: bfloat16 [64, 128, 256, 256], P('term', 'sector'), may hold values from -0.046875 to 0.046875
- targets: int32 [64, 128], P('term', 'sector'), may hold values from 0 to 127, as said below
Outputs:
- sigma: bfloat16 [2, 128, 256, 256], P(None, 'sector', 'term')
The draws below stay inside these ranges and needn't reach their ends.
Inputs may be any that keep to these rules, and one draw needn't show every extreme that they name: In each device block of targets (8 term groups by 4 source blocks, aligned), at most 2 entries fall into any one group of 4 consecutive target blocks (the blocks k * 4 to k * 4 + 3), and some group receives exactly 2 of them.
All inputs are finite; a program needn't handle non-finite values.
Results may differ from the reference program's by a relative error of at most 0.0049.
Values may be sent and summed in bfloat16 or wider, within the bound.
A program may use at most 192 MiB of HBM per device.

```python
import jax
import jax.numpy as jnp
from jax import lax

BLOCK = 256
SEC_DEV = 4
TERM_DEV = 8
BLOCKS = 128
TERMS = 64
CAPACITY = 2
N_SECTOR = 32
N_TERM = 8


def draw_targets(key, part):
    key = jax.random.fold_in(key, 7)
    per_block = TERM_DEV * SEC_DEV
    slot_count = N_SECTOR * CAPACITY

    def one_block(block_key):
        key_one, key_two, key_three, key_four = jax.random.split(block_key, 4)
        forced = jax.random.randint(key_one, (), 0, N_SECTOR)
        ranks = jax.random.permutation(key_two, slot_count).astype(jnp.int32)
        slot_ids = jnp.arange(slot_count, dtype=jnp.int32)
        scores = jnp.where(slot_ids // CAPACITY == forced, -slot_count + slot_ids % CAPACITY, ranks)
        chosen = jnp.argsort(scores, stable=True)[:per_block].astype(jnp.int32)
        chosen = jax.random.permutation(key_three, chosen)
        within = jax.random.randint(key_four, (per_block,), 0, SEC_DEV)
        return chosen // CAPACITY * SEC_DEV + within
    blocks = jax.vmap(one_block)(jax.random.split(key, N_TERM * N_SECTOR))
    blocks = blocks.reshape(N_TERM, N_SECTOR, TERM_DEV, SEC_DEV)
    return jnp.transpose(blocks, (0, 2, 1, 3)).reshape(TERMS, BLOCKS).astype(jnp.int32)


def levels(rng, shape, cuts, smallest, top_value):
    gain = 1.0
    for dim, blocks in cuts:
        draws = jax.random.uniform(jax.random.fold_in(jax.random.fold_in(rng, 6), dim), (blocks,), jnp.float32, smallest / len(cuts), top_value / len(cuts))
        gain = gain * jnp.repeat(jnp.exp(draws), shape[dim] // blocks).reshape((-1,) + (1,) * (len(shape) - 1 - dim))
    return gain


def noise(rng, shape, scale, bound, pieces=(), kind=jnp.bfloat16):
    result = scale * jax.random.normal(rng, shape, jnp.float32)
    if pieces:
        result = result * levels(rng, shape, pieces, -0.22, 0.18)
    return jnp.clip(result, -bound, bound).astype(kind)


def setup_inputs(seed: int = 0) -> dict:
    keys = jax.random.split(jax.random.key(seed), 5)
    wavefunction = noise(keys[0], (2, BLOCKS, BLOCK, BLOCK), 1.0, 6.0, ((1, 32),))
    left_ops = noise(keys[1], (TERMS, BLOCKS, BLOCK, BLOCK), BLOCK ** -0.5, 0.375, ((0, 8), (1, 32)))
    right_ops = noise(keys[2], (TERMS, BLOCKS, BLOCK, BLOCK), (BLOCK * TERMS) ** -0.5, 0.046875, ((0, 8), (1, 32)))
    targets = draw_targets(jax.random.fold_in(keys[4], 71), 0)
    return dict(wavefunction=wavefunction, left_ops=left_ops, right_ops=right_ops, targets=targets)


def reference(wavefunction, left_ops, right_ops, targets):
    wave_wide = wavefunction.astype(jnp.float32)

    def one_group(carry, inputs):
        left_group, right_group, target_row = inputs
        halves = jnp.einsum("sij,vsjk->vsik", left_group.astype(jnp.float32), wave_wide).astype(jnp.bfloat16)
        halves = lax.optimization_barrier(halves)
        right_sel = jnp.take(right_group, target_row.astype(jnp.int32), axis=0).astype(jnp.float32)
        products = jnp.einsum("vsij,sjk->vsik", halves.astype(jnp.float32), right_sel)
        summed = jax.ops.segment_sum(jnp.moveaxis(products, 1, 0), target_row.astype(jnp.int32), num_segments=BLOCKS)
        return carry + summed, None

    start = jnp.zeros((BLOCKS, 2, BLOCK, BLOCK), jnp.float32)
    total, unused = lax.scan(one_group, start, (left_ops, right_ops, targets))
    return jnp.moveaxis(total, 0, 1).astype(jnp.bfloat16)
```

```python
import jax
import jax.numpy as jnp
from jax import lax
from jax.experimental import pallas as pl
from jax.experimental.pallas import tpu as pltpu
from jax.sharding import PartitionSpec as P


def slot_rank(dest_row):
    count = dest_row.shape[0]
    same = dest_row[:, None] == dest_row[None, :]
    lower = jnp.arange(count)[None, :] < jnp.arange(count)[:, None]
    return jnp.sum((same & lower).astype(jnp.int32), axis=1)


def contract(wave_at, right_at, owner_at, valid, left_ref, wave_ref, right_ref, out_ref, acc):
    step = pl.program_id(0)

    @pl.when(step == 0)
    def _():
        acc[...] = jnp.zeros_like(acc)

    @pl.when(valid[step] > 0)
    def _():
        owner = owner_at[step]
        for v in range(2):
            half = jnp.dot(left_ref[0], wave_ref[v, 0], preferred_element_type=jnp.float32)
            half = half.astype(jnp.bfloat16)
            acc[v, owner] += jnp.dot(half, right_ref[0], preferred_element_type=jnp.float32)

    @pl.when(step == pl.num_programs(0) - 1)
    def _():
        out_ref[...] = acc[...].astype(out_ref.dtype)


def shards(wavefunction, left_ops, right_ops, targets):
    group_dev, sector_dev, width, unused = left_ops.shape
    per_dev = group_dev * sector_dev
    sectors = lax.axis_size("sector")
    terms = lax.axis_size("term")
    capacity = max(2, (2 * per_dev + sectors - 1) // sectors)
    slot_total = sectors * capacity
    my_index = lax.axis_index("sector")
    my_term = lax.axis_index("term")

    share = lax.dynamic_index_in_dim(
        wavefunction.reshape(2 * sector_dev, width, width), my_term, 0, keepdims=True
    )
    share = lax.all_gather(share, "sector", axis=0, tiled=True)
    wave_all = lax.all_gather(share, "term", axis=0, tiled=True)
    wave_all = wave_all.reshape(2, sector_dev * sectors, width, width)

    flat_targets = targets.reshape(per_dev)
    dest_dev = flat_targets // sector_dev
    send_slot = dest_dev * capacity + slot_rank(dest_dev)
    placing = (send_slot[None, :] == jnp.arange(slot_total)[:, None]).astype(jnp.int32)
    send_row = jnp.sum(placing * jnp.arange(per_dev, dtype=jnp.int32)[None, :], axis=1)
    send_buf = jnp.take(left_ops.reshape(per_dev, width, width), send_row, axis=0)
    left_all = lax.all_to_all(send_buf, "sector", split_axis=0, concat_axis=0, tiled=True)

    all_targets = lax.all_gather(targets.reshape(1, per_dev), "sector", axis=0, tiled=True)
    all_dest = all_targets // sector_dev
    all_rank = jax.vmap(slot_rank)(all_dest)
    match = (all_dest[:, None, :] == my_index) & (
        all_rank[:, None, :] == jnp.arange(capacity)[None, :, None]
    )
    match_int = match.astype(jnp.int32)
    valid = jnp.sum(match_int, axis=2).reshape(slot_total)
    source_row = jnp.sum(
        match_int * jnp.arange(per_dev, dtype=jnp.int32)[None, None, :], axis=2
    ).reshape(slot_total)
    owner = (jnp.sum(match_int * all_targets[:, None, :], axis=2) % sector_dev).reshape(slot_total)
    right_at = source_row // sector_dev * sector_dev + owner
    wave_at = source_row % sector_dev * sectors + jnp.arange(slot_total, dtype=jnp.int32) // capacity

    partial = pl.pallas_call(
        contract,
        out_shape=jax.ShapeDtypeStruct((2, sector_dev, width, width), jnp.bfloat16),
        grid_spec=pltpu.PrefetchScalarGridSpec(
            num_scalar_prefetch=4,
            grid=(slot_total,),
            in_specs=[
                pl.BlockSpec((1, width, width), lambda i, w, r, o, u: (i, 0, 0)),
                pl.BlockSpec((2, 1, width, width), lambda i, w, r, o, u: (0, w[i], 0, 0)),
                pl.BlockSpec((1, width, width), lambda i, w, r, o, u: (r[i], 0, 0)),
            ],
            out_specs=pl.BlockSpec((2, sector_dev, width, width), lambda i, w, r, o, u: (0, 0, 0, 0)),
            scratch_shapes=[pltpu.VMEM((2, sector_dev, width, width), jnp.float32)],
        ),
        compiler_params=pltpu.CompilerParams(vmem_limit_bytes=32 << 20),
    )(wave_at, right_at, owner, valid, left_all, wave_all, right_ops.reshape(per_dev, width, width))

    row_count = width // terms
    pieces = partial.reshape(2, sector_dev, terms, row_count, width)
    pieces = lax.all_to_all(pieces, "term", split_axis=2, concat_axis=2, tiled=True)
    return jnp.sum(pieces.astype(jnp.float32), axis=2).astype(jnp.bfloat16)


def solution(mesh):
    in_specs = (
        P(None, "sector", None, None),
        P("term", "sector", None, None),
        P("term", "sector", None, None),
        P("term", "sector"),
    )
    out_specs = P(None, "sector", "term", None)
    return jax.shard_map(shards, mesh=mesh, in_specs=in_specs, out_specs=out_specs, check_vma=False)
```

```python
import functools

import jax
import jax.numpy as jnp
from jax import lax
from jax.experimental import pallas as pl
from jax.experimental.pallas import tpu as pltpu
from jax.sharding import PartitionSpec as P

MESH = pl.DeviceIdType.MESH
NZ, NY, NX = 8, 4, 4
STEPS = [(dz, dy) for dy in (0, -1, 1, 2) for dz in (0, 4, 2, -2, 1, -1, 3, -3)]
ROWS = (0, 1, -1, 2)
WINDOW = 8


def slot_rank(dest_row):
    count = dest_row.shape[0]
    same = dest_row[:, None] == dest_row[None, :]
    lower = jnp.arange(count)[None, :] < jnp.arange(count)[:, None]
    return jnp.sum((same & lower).astype(jnp.int32), axis=1)


def place():
    sector, term = lax.axis_index("sector"), lax.axis_index("term")
    return sector // NY, lax.rem(sector, NY), term // 2, lax.rem(term, 2)


def shift(index, by, size):
    return lax.rem(index + by + size, size)


def exchange(send_row, left_ref, wave_ref, recv_ref, all_ref, send, own_sem, a2a_s, a2a_r, ring_s, ring_r,
             row_s, row_r, col_s, col_r, hand_s, hand_r, core_s, core_r):
    z, y, x, c = place()

    def device(dz=0, dy=0, dx=0, dc=0):
        return (shift(z, dz, NZ) * NY + shift(y, dy, NY), shift(x, dx, NX) * 2 + lax.rem(c + dc, 2))

    def term(dx):
        return shift(x, dx, NX) * 2 + c

    barrier = pltpu.get_barrier_semaphore()
    partners = [device(dz, dy) for dz, dy in STEPS[1:]] + [device(dx=1), device(dx=-1), device(dc=1)]
    for partner in partners:
        pl.semaphore_signal(barrier, inc=1, device_id=partner, device_id_type=MESH)
    pl.semaphore_wait(barrier, len(partners))

    def remote(src, dst, sems, where):
        copy = pltpu.make_async_remote_copy(src, dst, *sems, device_id=where, device_id_type=MESH)
        copy.start()
        return copy

    mine = x * 2 + c
    own = pltpu.make_async_copy(wave_ref.at[mine], all_ref.at[mine, y, z], own_sem.at[0])
    own.start()

    ring = {}

    def ring_step(sign, hop):
        k = hop - 1 + (4 if sign < 0 else 0)
        spot = all_ref.at[mine, y, shift(z, -sign * (hop - 1), NZ)]
        src = wave_ref.at[mine] if hop == 1 else spot
        ring[sign, hop] = remote(src, spot, (ring_s.at[k], ring_r.at[k]), device(dz=sign))

    a2a = []

    def send_left(k):
        dz, dy = STEPS[k]
        to = shift(z, dz, NZ) * NY + shift(y, dy, NY)
        for r in range(2):
            send[k, r] = left_ref[send_row[to * 2 + r]]
        if k == 0:
            copy = pltpu.make_async_copy(send.at[0], recv_ref.at[0], own_sem.at[1])
            copy.start()
        else:
            copy = remote(send.at[k], recv_ref.at[k], (a2a_s.at[k], a2a_r.at[k]), device(dz, dy))
        a2a.append(copy)

    def paced(k):
        if k > WINDOW:
            a2a[k - WINDOW].wait_send()
        send_left(k)

    ring_step(1, 1)
    ring_step(-1, 1)
    for k in range(4):
        send_left(k)
    for hop in (2, 3, 4):
        ring[1, hop - 1].wait_recv()
        ring_step(1, hop)
        if hop < 4:
            ring[-1, hop - 1].wait_recv()
            ring_step(-1, hop)
    ring[1, 4].wait_recv()
    ring[-1, 3].wait_recv()
    own.wait()

    rows, cols, hands, cores = [], [], [], []
    for i, dy in enumerate(ROWS[1:]):
        rows.append(remote(all_ref.at[mine, y], all_ref.at[mine, y], (row_s.at[i], row_r.at[i]), device(dy=-dy)))

    def along(q):
        if q:
            rows[q - 1].wait_recv()
        line = shift(y, ROWS[q], NY)
        for i, dx in enumerate((1, -1)):
            spot = all_ref.at[mine, line]
            cols.append(remote(spot, spot, (col_s.at[q, i], col_r.at[q, i]), device(dx=dx)))

    def hand_on(q):
        line = shift(y, ROWS[q], NY)
        for i, dx in enumerate((1, -1)):
            cols[2 * q + i].wait_recv()
            spot = all_ref.at[term(-dx), line, pl.ds(4 * i, 4)]
            hands.append(remote(spot, spot, (hand_s.at[q, i], hand_r.at[q, i]), device(dx=dx)))

    def across(q):
        line = shift(y, ROWS[q], NY)
        for i in range(2):
            hands[2 * q + i].wait_recv()
        for dx in range(NX):
            spot = all_ref.at[term(dx), line]
            cores.append(remote(spot, spot, (core_s.at[q, dx], core_r.at[q, dx]), device(dc=1)))

    along(0)
    for k in range(4, 12):
        paced(k)
    along(1)
    for k in range(12, 16):
        paced(k)
    along(2)
    hand_on(0)
    for k in range(16, 20):
        paced(k)
    along(3)
    across(0)
    hand_on(1)
    for k in range(20, 24):
        paced(k)
    across(1)
    hand_on(2)
    for k in range(24, 28):
        paced(k)
    across(2)
    hand_on(3)
    for k in range(28, 32):
        paced(k)
    across(3)

    for copy in cores:
        copy.wait()
    for copy in [*rows, *cols, *hands, *ring.values()]:
        copy.wait_send()
    a2a[0].wait()
    for k in range(1, 32):
        if k > 31 - WINDOW:
            a2a[k].wait_send()
        a2a[k].wait_recv()


def contract(wave_at, right_at, owner_at, valid, left_ref, wave_ref, right_ref, out_ref, acc):
    step = pl.program_id(0)

    @pl.when(step == 0)
    def _():
        acc[...] = jnp.zeros_like(acc)

    @pl.when(valid[step] > 0)
    def _():
        owner = owner_at[step]
        for v in range(2):
            half = jnp.dot(left_ref[0], wave_ref[v, 0], preferred_element_type=jnp.float32)
            half = half.astype(jnp.bfloat16)
            acc[v, owner] += jnp.dot(half, right_ref[0], preferred_element_type=jnp.float32)

    @pl.when(step == pl.num_programs(0) - 1)
    def _():
        out_ref[...] = acc[...].astype(out_ref.dtype)


def shards(wavefunction, left_ops, right_ops, targets):
    group_dev, sector_dev, width, unused = left_ops.shape
    per_dev = group_dev * sector_dev
    sectors = lax.axis_size("sector")
    terms = lax.axis_size("term")
    capacity = 2
    slot_total = sectors * capacity
    my_index = lax.axis_index("sector")
    z, y, x, c = place()

    flat_targets = targets.reshape(per_dev)
    all_targets = lax.all_gather(targets.reshape(1, per_dev), "sector", axis=0, tiled=True)
    dest_dev = flat_targets // sector_dev
    send_slot = dest_dev * capacity + slot_rank(dest_dev)
    placing = (send_slot[None, :] == jnp.arange(slot_total)[:, None]).astype(jnp.int32)
    send_row = jnp.sum(placing * jnp.arange(per_dev, dtype=jnp.int32)[None, :], axis=1)

    steps = jnp.array(STEPS, jnp.int32)
    source = shift(z, -steps[:, 0], NZ) * NY + shift(y, -steps[:, 1], NY)
    pick = (source[:, None] == jnp.arange(sectors)[None, :]).astype(jnp.int32)
    all_targets = jnp.sum(pick[:, :, None] * all_targets[None], axis=1)
    all_dest = all_targets // sector_dev
    all_rank = jax.vmap(slot_rank)(all_dest)
    match = (all_dest[:, None, :] == my_index) & (
        all_rank[:, None, :] == jnp.arange(capacity)[None, :, None]
    )
    match_int = match.astype(jnp.int32)
    valid = jnp.sum(match_int, axis=2).reshape(slot_total)
    source_row = jnp.sum(
        match_int * jnp.arange(per_dev, dtype=jnp.int32)[None, None, :], axis=2
    ).reshape(slot_total)
    owner = (jnp.sum(match_int * all_targets[:, None, :], axis=2) % sector_dev).reshape(slot_total)
    right_at = source_row // sector_dev * sector_dev + owner
    spot = lax.rem(source, NY) * NZ + source // NY
    wave_at = source_row % sector_dev * sectors + jnp.repeat(spot, capacity)

    block = (width, width)
    hbm = pl.BlockSpec(memory_space=pl.ANY)
    dma = pltpu.SemaphoreType.DMA
    left_all, wave_all = pl.pallas_call(
        exchange,
        out_shape=(
            jax.ShapeDtypeStruct((sectors, capacity, *block), jnp.bfloat16),
            jax.ShapeDtypeStruct((terms, NY, NZ, *block), jnp.bfloat16),
        ),
        in_specs=[
            pl.BlockSpec(memory_space=pltpu.SMEM),
            pl.BlockSpec(memory_space=pltpu.VMEM),
            hbm,
        ],
        out_specs=(hbm, hbm),
        scratch_shapes=[
            pltpu.VMEM((sectors, capacity, *block), jnp.bfloat16),
            dma((2,)),
            dma((32,)), dma((32,)), dma((8,)), dma((8,)), dma((3,)), dma((3,)),
            dma((4, 2)), dma((4, 2)), dma((4, 2)), dma((4, 2)), dma((4, 4)), dma((4, 4)),
        ],
        compiler_params=pltpu.CompilerParams(
            collective_id=0, has_side_effects=True, vmem_limit_bytes=40 << 20
        ),
    )(send_row, left_ops.reshape(per_dev, *block), wavefunction.reshape(2 * sector_dev, *block))
    left_all = left_all.reshape(slot_total, *block)
    wave_all = wave_all.reshape(2, sector_dev * sectors, *block)

    partial = pl.pallas_call(
        contract,
        out_shape=jax.ShapeDtypeStruct((2, sector_dev, width, width), jnp.bfloat16),
        grid_spec=pltpu.PrefetchScalarGridSpec(
            num_scalar_prefetch=4,
            grid=(slot_total,),
            in_specs=[
                pl.BlockSpec((1, width, width), lambda i, w, r, o, u: (i, 0, 0)),
                pl.BlockSpec((2, 1, width, width), lambda i, w, r, o, u: (0, w[i], 0, 0)),
                pl.BlockSpec((1, width, width), lambda i, w, r, o, u: (r[i], 0, 0)),
            ],
            out_specs=pl.BlockSpec((2, sector_dev, width, width), lambda i, w, r, o, u: (0, 0, 0, 0)),
            scratch_shapes=[pltpu.VMEM((2, sector_dev, width, width), jnp.float32)],
        ),
        compiler_params=pltpu.CompilerParams(vmem_limit_bytes=32 << 20),
    )(wave_at, right_at, owner, valid, left_all, wave_all, right_ops.reshape(per_dev, *block))

    row_count = width // terms
    pieces = partial.reshape(2, sector_dev, terms, row_count, width)
    pieces = lax.all_to_all(pieces, "term", split_axis=2, concat_axis=2, tiled=True)
    return jnp.sum(pieces.astype(jnp.float32), axis=2).astype(jnp.bfloat16)


def solution(mesh):
    in_specs = (
        P(None, "sector", None, None),
        P("term", "sector", None, None),
        P("term", "sector", None, None),
        P("term", "sector"),
    )
    out_specs = P(None, "sector", "term", None)
    return jax.shard_map(shards, mesh=mesh, in_specs=in_specs, out_specs=out_specs, check_vma=False)
```

```python
import jax
import jax.numpy as jnp
from jax import lax
from jax.experimental import pallas as pl
from jax.experimental.pallas import tpu as pltpu
from jax.sharding import PartitionSpec as P

MESH = pl.DeviceIdType.MESH
NZ, NY, NX = 8, 4, 4
STEPS = [(dz, dy) for dy in (0, -1, 1, 2) for dz in (0, 4, 2, -2, 1, -1, 3, -3)]
ROWS = (0, 1, -1, 2)
WINDOW = 8


def slot_rank(dest_row):
    count = dest_row.shape[0]
    same = dest_row[:, None] == dest_row[None, :]
    lower = jnp.arange(count)[None, :] < jnp.arange(count)[:, None]
    return jnp.sum((same & lower).astype(jnp.int32), axis=1)


def place():
    sector, term = lax.axis_index("sector"), lax.axis_index("term")
    return sector // NY, lax.rem(sector, NY), term // 2, lax.rem(term, 2)


def shift(index, by, size):
    return lax.rem(index + by + size, size)


def contract_all(code_ref, meta_ref, left_ref, right_ref, wave_ref, out_ref, all_ref, send, recv, meta_got, meta_at, stage, halves,
                 picked, acc, pair, half_sum, got, own_sem, stage_sem, a2a_s, a2a_r, meta_s, meta_r, ring_s, ring_r,
                 row_s, row_r, col_s, col_r, hand_s, hand_r, core_s, core_r, pair_s, pair_r, sum_s, sum_r):
    z, y, x, c = place()
    width = left_ref.shape[-1]

    def device(dz=0, dy=0, dx=0, dc=0):
        return (shift(z, dz, NZ) * NY + shift(y, dy, NY), shift(x, dx, NX) * 2 + lax.rem(c + dc, 2))

    def term(dx):
        return shift(x, dx, NX) * 2 + c

    barrier = pltpu.get_barrier_semaphore()
    partners = [device(dz, dy) for dz, dy in STEPS[1:]] + [device(dx=dx) for dx in (1, -1, 2)] + [device(dc=1)]
    for partner in partners:
        pl.semaphore_signal(barrier, inc=1, device_id=partner, device_id_type=MESH)
    pl.semaphore_wait(barrier, len(partners))

    def remote(src, dst, sems, where):
        copy = pltpu.make_async_remote_copy(src, dst, *sems, device_id=where, device_id_type=MESH)
        copy.start()
        return copy

    mine = x * 2 + c
    own = pltpu.make_async_copy(wave_ref.at[mine], all_ref.at[mine, y, z], own_sem.at[0])
    own.start()

    ring = {}

    def ring_step(sign, hop):
        k = hop - 1 + (4 if sign < 0 else 0)
        spot = all_ref.at[mine, y, shift(z, -sign * (hop - 1), NZ)]
        src = wave_ref.at[mine] if hop == 1 else spot
        ring[sign, hop] = remote(src, spot, (ring_s.at[k], ring_r.at[k]), device(dz=sign))

    a2a = []
    metas = []

    def owner_of(k):
        dz, dy = STEPS[k]
        return shift(z, dz, NZ) * NY + shift(y, dy, NY)

    def send_meta(k):
        src, dst = meta_ref.at[owner_of(k)], meta_got.at[k]
        if k == 0:
            copy = pltpu.make_async_copy(src, dst, own_sem.at[1])
            copy.start()
        else:
            copy = remote(src, dst, (meta_s.at[k], meta_r.at[k]), device(*STEPS[k]))
        metas.append(copy)

    def send_left(k):
        to = owner_of(k)
        buf = recv if k == 0 else send
        for r in range(2):
            buf[k, r] = left_ref[code_ref[to, 0, r] // 8]
        a2a.append(k and remote(send.at[k], recv.at[k], (a2a_s.at[k], a2a_r.at[k]), device(*STEPS[k])))

    def paced(first, last):
        for k in range(first, last):
            if k > WINDOW:
                a2a[k - WINDOW].wait_send()
            send_left(k)

    ring_step(1, 1)
    ring_step(-1, 1)
    for k in range(4):
        send_left(k)
    for k in range(32):
        send_meta(k)
    acc[...] = jnp.zeros_like(acc)
    for hop in (2, 3, 4):
        ring[1, hop - 1].wait_recv()
        ring_step(1, hop)
        if hop < 4:
            ring[-1, hop - 1].wait_recv()
            ring_step(-1, hop)
    ring[1, 4].wait_recv()
    ring[-1, 3].wait_recv()
    own.wait()

    rows, cols, hands, cores = [], [], [], []
    for i, dy in enumerate(ROWS[1:]):
        rows.append(remote(all_ref.at[mine, y], all_ref.at[mine, y], (row_s.at[i], row_r.at[i]), device(dy=-dy)))

    def along(q):
        if q:
            rows[q - 1].wait_recv()
        line = shift(y, ROWS[q], NY)
        for i, dx in enumerate((1, -1)):
            spot = all_ref.at[mine, line]
            cols.append(remote(spot, spot, (col_s.at[q, i], col_r.at[q, i]), device(dx=dx)))

    def hand_on(q):
        line = shift(y, ROWS[q], NY)
        for i, dx in enumerate((1, -1)):
            cols[2 * q + i].wait_recv()
            spot = all_ref.at[term(-dx), line, pl.ds(4 * i, 4)]
            hands.append(remote(spot, spot, (hand_s.at[q, i], hand_r.at[q, i]), device(dx=dx)))

    def across(q):
        line = shift(y, ROWS[q], NY)
        for i in range(2):
            hands[2 * q + i].wait_recv()
        for dx in range(NX):
            spot = all_ref.at[term(dx), line]
            cores.append(remote(spot, spot, (core_s.at[q, dx], core_r.at[q, dx]), device(dc=1)))

    def group(g):
        if g % 2 == 0:
            for copy in cores[2 * g : 2 * g + 4]:
                copy.wait_recv()
        loads = []
        for i in range(4):
            dz, dy = STEPS[4 * g + i]
            copy = pltpu.make_async_copy(all_ref.at[:, shift(y, -dy, NY), shift(z, -dz, NZ)], stage.at[i], stage_sem.at[i])
            copy.start()
            loads.append(copy)
        for copy in loads:
            copy.wait()
        for k in range(max(4 * g, 1), 4 * g + 4):
            a2a[k].wait_recv()

        def slot(j, carry):
            i, r = j // 2, lax.rem(j, 2)
            code = meta_at[4 * g + i, 0, r]
            live, owner, source = lax.rem(code, 2), lax.rem(code // 2, 4), lax.rem(code // 8, 4)
            left = recv[4 * g + i, r]
            span = pl.ds(pl.multiple_of(j * width, width), width)
            for v in range(2):
                half = jnp.dot(left, stage[i, v * 4 + source], preferred_element_type=jnp.float32)
                halves[v * width : (v + 1) * width, span] = half.astype(halves.dtype)
            right = right_ref[code // 32 * 4 + owner]
            for b in range(4):
                keep = (live > 0) & (owner == b)
                picked[b, span, :] = jnp.where(keep, right, jnp.zeros_like(right))
            return carry

        def block(b, carry):
            product = jnp.dot(halves[...], picked[b], preferred_element_type=jnp.float32)
            for v in range(2):
                for t in range(8):
                    at = v * width + t * 32
                    acc[t % 2, t // 2, v, b] += product[at : at + 32]
            return carry

        lax.fori_loop(0, 8, slot, 0)
        lax.fori_loop(0, 4, block, 0)

    along(0)
    paced(4, 12)
    for copy in metas:
        copy.wait() if copy is metas[0] else copy.wait_recv()
    table = pltpu.make_async_copy(meta_got, meta_at, own_sem.at[2])
    table.start()
    along(1)
    paced(12, 16)
    along(2)
    hand_on(0)
    paced(16, 20)
    along(3)
    across(0)
    hand_on(1)
    paced(20, 24)
    across(1)
    table.wait()
    group(0)
    hand_on(2)
    paced(24, 26)
    group(1)
    paced(26, 28)
    across(2)
    group(2)
    hand_on(3)
    paced(28, 30)
    group(3)
    paced(30, 32)
    across(3)
    for g in range(4, 8):
        group(g)

    order = (1, -1, 2, 0)
    pairs, sums = [], []
    for i, dx in enumerate(order):
        pairs.append(remote(acc.at[1 - c, shift(x, dx, NX)], pair.at[i], (pair_s.at[i], pair_r.at[i]), device(dc=1)))
    for i, dx in enumerate(order[:3]):
        pairs[i].wait_recv()
        half_sum[i] = (acc[c, shift(x, dx, NX)] + pair[i]).astype(half_sum.dtype)
        sums.append(remote(half_sum.at[i], got.at[i], (sum_s.at[i], sum_r.at[i]), device(dx=dx)))
    pairs[3].wait_recv()
    total = acc[c, x] + pair[3]
    for i in range(3):
        sums[i].wait_recv()
        total += got[i].astype(jnp.float32)
    out_ref[...] = total.astype(out_ref.dtype)

    for copy in [*rows, *cols, *hands, *cores, *ring.values(), *metas[1:], *a2a[32 - WINDOW :], *pairs, *sums]:
        copy.wait_send()


def shards(wavefunction, left_ops, right_ops, targets):
    group_dev, sector_dev, width, unused = left_ops.shape
    per_dev = group_dev * sector_dev
    sectors = lax.axis_size("sector")
    terms = lax.axis_size("term")
    capacity = 2

    flat_targets = targets.reshape(per_dev)
    dest_dev = flat_targets // sector_dev
    send_slot = dest_dev * capacity + slot_rank(dest_dev)
    lane = jnp.arange(sectors * capacity)
    code = (jnp.arange(per_dev, dtype=jnp.int32) * 4 + flat_targets % sector_dev) * 2 + 1
    code = jnp.sum(jnp.where(send_slot[None, :] == lane[:, None], code[None, :], 0), axis=1)
    code = jnp.pad(code.reshape(sectors, 1, capacity), ((0, 0), (0, 0), (0, 128 - capacity)))

    block = (width, width)
    hbm = pl.BlockSpec(memory_space=pl.ANY)
    vmem = pl.BlockSpec(memory_space=pltpu.VMEM)
    dma = pltpu.SemaphoreType.DMA
    low, wide = jnp.bfloat16, jnp.float32
    piece = (2, sector_dev, width // terms, width)
    out, unused = pl.pallas_call(
        contract_all,
        out_shape=(
            jax.ShapeDtypeStruct(piece, low),
            jax.ShapeDtypeStruct((terms, NY, NZ, *block), low),
        ),
        in_specs=[pl.BlockSpec(memory_space=pltpu.SMEM), vmem, vmem, vmem, hbm],
        out_specs=(vmem, hbm),
        scratch_shapes=[
            pltpu.VMEM((sectors, capacity, *block), low),
            pltpu.VMEM((sectors, capacity, *block), low),
            pltpu.VMEM((sectors, 1, 128), jnp.int32),
            pltpu.SMEM((sectors, 1, 128), jnp.int32),
            pltpu.VMEM((4, terms, *block), low),
            pltpu.VMEM((2 * width, 8 * width), low),
            pltpu.VMEM((4, 8 * width, width), low),
            pltpu.VMEM((2, NX, *piece), wide),
            pltpu.VMEM((NX, *piece), wide),
            pltpu.VMEM((3, *piece), low),
            pltpu.VMEM((3, *piece), low),
            dma((3,)), dma((4,)),
            dma((32,)), dma((32,)), dma((32,)), dma((32,)), dma((8,)), dma((8,)), dma((3,)), dma((3,)),
            dma((4, 2)), dma((4, 2)), dma((4, 2)), dma((4, 2)), dma((4, 4)), dma((4, 4)),
            dma((4,)), dma((4,)), dma((3,)), dma((3,)),
        ],
        compiler_params=pltpu.CompilerParams(
            collective_id=0, has_side_effects=True, vmem_limit_bytes=56 << 20
        ),
    )(
        code, code, left_ops.reshape(per_dev, *block), right_ops.reshape(per_dev, *block),
        wavefunction.reshape(2 * sector_dev, *block),
    )
    return out


def solution(mesh):
    in_specs = (
        P(None, "sector", None, None),
        P("term", "sector", None, None),
        P("term", "sector", None, None),
        P("term", "sector"),
    )
    out_specs = P(None, "sector", "term", None)
    return jax.shard_map(shards, mesh=mesh, in_specs=in_specs, out_specs=out_specs, check_vma=False)
```

```python
import jax
import jax.numpy as jnp
from jax import lax
from jax.experimental import pallas as pl
from jax.experimental.pallas import tpu as pltpu
from jax.sharding import PartitionSpec as P

MESH = pl.DeviceIdType.MESH
NZ, NY, NX = 8, 4, 4
STEPS = [(dz, dy) for pair in ((0, 2), (-1, 1)) for dz in (0, 4, 3, -3, 2, -2, 1, -1) for dy in pair]
ROWS = (0, 2, 1, -1)
NEAR = (0, 1, -1, 2, -2, 3, -3, 4)
WINDOW = 16
EARLY = 4
PLAN = [
    ("send", 4, 8), ("along", 1), ("table",), ("send", 8, 12), ("hand", 0), ("along", 2), ("send", 12, 16),
    ("cross", 0), ("hand", 1), ("along", 3), ("send", 16, 20), ("cross", 1), ("hand", 2), ("send", 20, 24),
    ("group", 0), ("group", 1), ("cross", 2), ("hand", 3), ("send", 24, 28), ("group", 2), ("cross", 3),
    ("group", 3), ("send", 28, 32), ("group", 4), ("group", 5), ("group", 6), ("group", 7),
]


def slot_rank(dest_row):
    count = dest_row.shape[0]
    same = dest_row[:, None] == dest_row[None, :]
    lower = jnp.arange(count)[None, :] < jnp.arange(count)[:, None]
    return jnp.sum((same & lower).astype(jnp.int32), axis=1)


def place():
    sector, term = lax.axis_index("sector"), lax.axis_index("term")
    return sector // NY, lax.rem(sector, NY), term // 2, lax.rem(term, 2)


def shift(index, by, size):
    return lax.rem(index + by + size, size)


def contract_all(code_ref, meta_ref, left_hbm, right_hbm, wave_ref, out_ref, all_ref, left_ref, right_ref, send, recv, meta_got, meta_at, stage, halves,
                 picked, acc, pair, half_sum, got, own_sem, stage_sem, a2a_s, a2a_r, meta_s, meta_r, ring_s, ring_r,
                 row_s, row_r, near_s, near_r, col_s, col_r, hand_s, hand_r, core_s, core_r, pair_s, pair_r, sum_s, sum_r):
    z, y, x, c = place()
    width = left_ref.shape[-1]
    left_load = pltpu.make_async_copy(left_hbm, left_ref, own_sem.at[3])
    left_load.start()
    right_load = pltpu.make_async_copy(right_hbm, right_ref, own_sem.at[4])

    def device(dz=0, dy=0, dx=0, dc=0):
        return (shift(z, dz, NZ) * NY + shift(y, dy, NY), shift(x, dx, NX) * 2 + lax.rem(c + dc, 2))

    def term(dx):
        return shift(x, dx, NX) * 2 + c

    barrier = pltpu.get_barrier_semaphore()
    partners = [device(dz, dy) for dz, dy in STEPS[1:]] + [device(dx=dx) for dx in (1, -1, 2)] + [device(dc=1)]
    for partner in partners:
        pl.semaphore_signal(barrier, inc=1, device_id=partner, device_id_type=MESH)
    pl.semaphore_wait(barrier, len(partners))

    def remote(src, dst, sems, where):
        copy = pltpu.make_async_remote_copy(src, dst, *sems, device_id=where, device_id_type=MESH)
        copy.start()
        return copy

    mine = x * 2 + c
    own = pltpu.make_async_copy(wave_ref.at[mine], all_ref.at[mine, y, z], own_sem.at[0])
    own.start()

    ring, rows, cols = {}, {}, {}

    def ring_step(sign, hop):
        k = hop - 1 + (4 if sign < 0 else 0)
        spot = all_ref.at[mine, y, shift(z, -sign * (hop - 1), NZ)]
        src = wave_ref.at[mine] if hop == 1 else spot
        ring[sign, hop] = remote(src, spot, (ring_s.at[k], ring_r.at[k]), device(dz=sign))

    def spread(dz):
        spot = all_ref.at[mine, y, shift(z, dz, NZ)]
        src = spot if dz else wave_ref.at[mine]
        j = NEAR.index(dz)
        for i, dx in enumerate((1, -1)):
            cols[0, i, j] = remote(src, spot, (near_s.at[i, j], near_r.at[i, j]), device(dx=dx))
        for i, dy in enumerate(ROWS[1:]):
            rows[i, j] = remote(src, spot, (row_s.at[i, j], row_r.at[i, j]), device(dy=-dy))

    a2a = []
    metas = []

    def owner_of(k):
        dz, dy = STEPS[k]
        return shift(z, dz, NZ) * NY + shift(y, dy, NY)

    def send_meta(k):
        src, dst = meta_ref.at[owner_of(k)], meta_got.at[k]
        if k == 0:
            copy = pltpu.make_async_copy(src, dst, own_sem.at[1])
            copy.start()
        else:
            copy = remote(src, dst, (meta_s.at[k], meta_r.at[k]), device(*STEPS[k]))
        metas.append(copy)

    def send_left(k):
        to = owner_of(k)
        buf = recv if k == 0 else send
        for r in range(2):
            buf[k, r] = left_ref[code_ref[to, 0, r] // 8]
        a2a.append(k and remote(send.at[k], recv.at[k], (a2a_s.at[k], a2a_r.at[k]), device(*STEPS[k])))

    def paced(first, last):
        for k in range(first, last):
            if k > WINDOW:
                a2a[k - WINDOW].wait_send()
            send_left(k)

    ring_step(1, 1)
    ring_step(-1, 1)
    spread(0)
    left_load.wait()
    right_load.start()
    for k in range(EARLY):
        send_left(k)
    for k in range(32):
        send_meta(k)
    acc[...] = jnp.zeros_like(acc)
    for hop in (1, 2, 3, 4):
        for sign in (1, -1):
            if sign > 0 or hop < 4:
                ring[sign, hop].wait_recv()
                if hop < (4 if sign > 0 else 3):
                    ring_step(sign, hop + 1)
                spread(-sign * hop if hop < 4 else 4)
    own.wait()
    right_load.wait()

    hands, cores = {}, {}

    def along(q):
        line = shift(y, ROWS[q], NY)
        for j in range(NZ):
            rows[q - 1, j].wait_recv()
        for i, dx in enumerate((1, -1)):
            spot = all_ref.at[mine, line]
            cols[q, i] = remote(spot, spot, (col_s.at[q, i], col_r.at[q, i]), device(dx=dx))

    def hand_on(q):
        line = shift(y, ROWS[q], NY)
        for i, dx in enumerate((1, -1)):
            if q:
                cols[q, i].wait_recv()
            else:
                for j in range(NZ):
                    cols[0, i, j].wait_recv()
            spot = all_ref.at[term(-dx), line, pl.ds(4 * i, 4)]
            hands[q, i] = remote(spot, spot, (hand_s.at[q, i], hand_r.at[q, i]), device(dx=dx))

    def across(q):
        line = shift(y, ROWS[q], NY)
        for i in range(2):
            hands[q, i].wait_recv()
        for dx in range(NX):
            spot = all_ref.at[term(dx), line]
            cores[q, dx] = remote(spot, spot, (core_s.at[q, dx], core_r.at[q, dx]), device(dc=1))

    table = []

    def read_table():
        for copy in metas:
            copy.wait() if copy is metas[0] else copy.wait_recv()
        copy = pltpu.make_async_copy(meta_got, meta_at, own_sem.at[2])
        copy.start()
        table.append(copy)

    def group(g):
        if g == 0:
            table[0].wait()
        if g % 4 == 0:
            for q in (g // 2, g // 2 + 1):
                for dx in range(NX):
                    cores[q, dx].wait_recv()
        loads = []
        for i in range(4):
            dz, dy = STEPS[4 * g + i]
            copy = pltpu.make_async_copy(all_ref.at[:, shift(y, -dy, NY), shift(z, -dz, NZ)], stage.at[i], stage_sem.at[i])
            copy.start()
            loads.append(copy)
        for copy in loads:
            copy.wait()
        for k in range(max(4 * g, 1), 4 * g + 4):
            a2a[k].wait_recv()

        def slot(j, carry):
            i, r = j // 2, lax.rem(j, 2)
            code = meta_at[4 * g + i, 0, r]
            live, owner, source = lax.rem(code, 2), lax.rem(code // 2, 4), lax.rem(code // 8, 4)
            left = recv[4 * g + i, r]
            span = pl.ds(pl.multiple_of(j * width, width), width)
            for v in range(2):
                half = jnp.dot(left, stage[i, v * 4 + source], preferred_element_type=jnp.float32)
                halves[v * width : (v + 1) * width, span] = half.astype(halves.dtype)
            right = right_ref[code // 32 * 4 + owner]
            for b in range(4):
                keep = (live > 0) & (owner == b)
                picked[b, span, :] = jnp.where(keep, right, jnp.zeros_like(right))
            return carry

        def block(b, carry):
            product = jnp.dot(halves[...], picked[b], preferred_element_type=jnp.float32)
            for v in range(2):
                for t in range(8):
                    at = v * width + t * 32
                    acc[t % 2, t // 2, v, b] += product[at : at + 32]
            return carry

        lax.fori_loop(0, 8, slot, 0)
        lax.fori_loop(0, 4, block, 0)

    def send_on(first, last):
        paced(max(first, EARLY), last)

    run = dict(send=send_on, table=read_table, along=along, hand=hand_on, cross=across, group=group)
    for kind, *rest in PLAN:
        run[kind](*rest)

    order = (1, -1, 2, 0)
    pairs, sums = [], []
    for i, dx in enumerate(order):
        pairs.append(remote(acc.at[1 - c, shift(x, dx, NX)], pair.at[i], (pair_s.at[i], pair_r.at[i]), device(dc=1)))
    for i, dx in enumerate(order[:3]):
        pairs[i].wait_recv()
        half_sum[i] = (acc[c, shift(x, dx, NX)] + pair[i]).astype(half_sum.dtype)
        sums.append(remote(half_sum.at[i], got.at[i], (sum_s.at[i], sum_r.at[i]), device(dx=dx)))
    pairs[3].wait_recv()
    total = acc[c, x] + pair[3]
    for i in range(3):
        sums[i].wait_recv()
        total += got[i].astype(jnp.float32)
    out_ref[...] = total.astype(out_ref.dtype)

    for group_of in (rows, cols, hands, cores, ring):
        for copy in group_of.values():
            copy.wait_send()
    for copy in [*metas[1:], *a2a[max(32 - WINDOW, 1) :], *pairs, *sums]:
        copy.wait_send()


def shards(wavefunction, left_ops, right_ops, targets):
    group_dev, sector_dev, width, unused = left_ops.shape
    per_dev = group_dev * sector_dev
    sectors = lax.axis_size("sector")
    terms = lax.axis_size("term")
    capacity = 2

    flat_targets = targets.reshape(per_dev)
    dest_dev = flat_targets // sector_dev
    send_slot = dest_dev * capacity + slot_rank(dest_dev)
    lane = jnp.arange(sectors * capacity)
    code = (jnp.arange(per_dev, dtype=jnp.int32) * 4 + flat_targets % sector_dev) * 2 + 1
    code = jnp.sum(jnp.where(send_slot[None, :] == lane[:, None], code[None, :], 0), axis=1)
    code = jnp.pad(code.reshape(sectors, 1, capacity), ((0, 0), (0, 0), (0, 128 - capacity)))

    block = (width, width)
    hbm = pl.BlockSpec(memory_space=pl.ANY)
    vmem = pl.BlockSpec(memory_space=pltpu.VMEM)
    dma = pltpu.SemaphoreType.DMA
    low, wide = jnp.bfloat16, jnp.float32
    piece = (2, sector_dev, width // terms, width)
    out, unused = pl.pallas_call(
        contract_all,
        out_shape=(
            jax.ShapeDtypeStruct(piece, low),
            jax.ShapeDtypeStruct((terms, NY, NZ, *block), low),
        ),
        in_specs=[pl.BlockSpec(memory_space=pltpu.SMEM), vmem, hbm, hbm, hbm],
        out_specs=(vmem, hbm),
        scratch_shapes=[
            pltpu.VMEM((per_dev, *block), low),
            pltpu.VMEM((per_dev, *block), low),
            pltpu.VMEM((sectors, capacity, *block), low),
            pltpu.VMEM((sectors, capacity, *block), low),
            pltpu.VMEM((sectors, 1, 128), jnp.int32),
            pltpu.SMEM((sectors, 1, 128), jnp.int32),
            pltpu.VMEM((4, terms, *block), low),
            pltpu.VMEM((2 * width, 8 * width), low),
            pltpu.VMEM((4, 8 * width, width), low),
            pltpu.VMEM((2, NX, *piece), wide),
            pltpu.VMEM((NX, *piece), wide),
            pltpu.VMEM((3, *piece), low),
            pltpu.VMEM((3, *piece), low),
            dma((5,)), dma((4,)),
            dma((32,)), dma((32,)), dma((32,)), dma((32,)), dma((8,)), dma((8,)), dma((3, 8)), dma((3, 8)), dma((2, 8)), dma((2, 8)),
            dma((4, 2)), dma((4, 2)), dma((4, 2)), dma((4, 2)), dma((4, 4)), dma((4, 4)),
            dma((4,)), dma((4,)), dma((3,)), dma((3,)),
        ],
        compiler_params=pltpu.CompilerParams(
            collective_id=0, has_side_effects=True, vmem_limit_bytes=56 << 20
        ),
    )(
        code, code, left_ops.reshape(per_dev, *block), right_ops.reshape(per_dev, *block),
        wavefunction.reshape(2 * sector_dev, *block),
    )
    return out


def solution(mesh):
    in_specs = (
        P(None, "sector", None, None),
        P("term", "sector", None, None),
        P("term", "sector", None, None),
        P("term", "sector"),
    )
    out_specs = P(None, "sector", "term", None)
    return jax.shard_map(shards, mesh=mesh, in_specs=in_specs, out_specs=out_specs, check_vma=False)
```

```python
import jax
import jax.numpy as jnp
from jax import lax
from jax.experimental import pallas as pl
from jax.experimental.pallas import tpu as pltpu
from jax.sharding import PartitionSpec as P

MESH = pl.DeviceIdType.MESH
NZ, NY, NX = 8, 4, 4
STEPS = [(dz, dy) for pair in ((0, 2), (-1, 1)) for dz in (0, 4, 3, -3, 2, -2, 1, -1) for dy in pair]
ROWS = (0, 2, 1, -1)
NEAR = (0, 1, -1, 2, -2, 3, -3, 4)
WINDOW = 16
EARLY = 4
SLOT_UNROLL = 4
BLOCK_UNROLL = 2
PLAN = [
    ("send", 0, 8), ("along", 1), ("table",), ("send", 8, 12), ("hand", 0), ("along", 2), ("send", 12, 16),
    ("cross", 0), ("hand", 1), ("along", 3), ("send", 16, 20), ("cross", 1), ("hand", 2), ("send", 20, 24),
    ("group", 0), ("group", 1), ("cross", 2), ("hand", 3), ("send", 24, 28), ("group", 2), ("cross", 3),
    ("group", 3), ("send", 28, 32), ("group", 4), ("group", 5), ("group", 6), ("group", 7),
]


def slot_rank(dest_row):
    count = dest_row.shape[0]
    same = dest_row[:, None] == dest_row[None, :]
    lower = jnp.arange(count)[None, :] < jnp.arange(count)[:, None]
    return jnp.sum((same & lower).astype(jnp.int32), axis=1)


def place():
    sector, term = lax.axis_index("sector"), lax.axis_index("term")
    return sector // NY, lax.rem(sector, NY), term // 2, lax.rem(term, 2)


def shift(index, by, size):
    return lax.rem(index + by + size, size)


def contract_all(code_ref, meta_ref, left_hbm, right_hbm, wave_ref, out_ref, all_ref, left_ref, right_ref, send, recv, meta_got, meta_at, stage_even, stage_odd, halves,
                 picked, acc, pair, half_sum, got, own_sem, stage_sem, a2a_s, a2a_r, meta_s, meta_r, ring_s, ring_r,
                 row_s, row_r, near_s, near_r, col_s, col_r, hand_s, hand_r, core_s, core_r, pair_s, pair_r, sum_s, sum_r):
    z, y, x, c = place()
    width = left_ref.shape[-1]
    left_load = pltpu.make_async_copy(left_hbm, left_ref, own_sem.at[3])
    left_load.start()
    right_load = pltpu.make_async_copy(right_hbm, right_ref, own_sem.at[4])

    def device(dz=0, dy=0, dx=0, dc=0):
        return (shift(z, dz, NZ) * NY + shift(y, dy, NY), shift(x, dx, NX) * 2 + lax.rem(c + dc, 2))

    def term(dx):
        return shift(x, dx, NX) * 2 + c

    barrier = pltpu.get_barrier_semaphore()
    partners = [device(dz, dy) for dz, dy in STEPS[1:]] + [device(dx=dx) for dx in (1, -1, 2)] + [device(dc=1)]
    for partner in partners:
        pl.semaphore_signal(barrier, inc=1, device_id=partner, device_id_type=MESH)

    def owner_of(k):
        dz, dy = STEPS[k]
        return shift(z, dz, NZ) * NY + shift(y, dy, NY)

    def pack(k):
        buf = recv if k == 0 else send
        for r in range(2):
            buf[k, r] = left_ref[code_ref[owner_of(k), 0, r] // 8]

    left_load.wait()
    for k in range(EARLY):
        pack(k)
    pl.semaphore_wait(barrier, len(partners))

    def remote(src, dst, sems, where):
        copy = pltpu.make_async_remote_copy(src, dst, *sems, device_id=where, device_id_type=MESH)
        copy.start()
        return copy

    mine = x * 2 + c
    own = pltpu.make_async_copy(wave_ref.at[mine], all_ref.at[mine, y, z], own_sem.at[0])
    own.start()

    ring, rows, cols = {}, {}, {}

    def ring_step(sign, hop):
        k = hop - 1 + (4 if sign < 0 else 0)
        spot = all_ref.at[mine, y, shift(z, -sign * (hop - 1), NZ)]
        src = wave_ref.at[mine] if hop == 1 else spot
        ring[sign, hop] = remote(src, spot, (ring_s.at[k], ring_r.at[k]), device(dz=sign))

    def spread(dz):
        spot = all_ref.at[mine, y, shift(z, dz, NZ)]
        src = spot if dz else wave_ref.at[mine]
        j = NEAR.index(dz)
        for i, dx in enumerate((1, -1)):
            cols[0, i, j] = remote(src, spot, (near_s.at[i, j], near_r.at[i, j]), device(dx=dx))
        for i, dy in enumerate(ROWS[1:]):
            rows[i, j] = remote(src, spot, (row_s.at[i, j], row_r.at[i, j]), device(dy=-dy))

    a2a = []
    metas = []

    def send_meta(k):
        src, dst = meta_ref.at[owner_of(k)], meta_got.at[k]
        if k == 0:
            copy = pltpu.make_async_copy(src, dst, own_sem.at[1])
            copy.start()
        else:
            copy = remote(src, dst, (meta_s.at[k], meta_r.at[k]), device(*STEPS[k]))
        metas.append(copy)

    def send_left(k):
        if k >= EARLY:
            pack(k)
        a2a.append(k and remote(send.at[k], recv.at[k], (a2a_s.at[k], a2a_r.at[k]), device(*STEPS[k])))

    def paced(first, last):
        for k in range(first, last):
            if k > WINDOW:
                a2a[k - WINDOW].wait_send()
            send_left(k)

    ring_step(1, 1)
    ring_step(-1, 1)
    spread(0)
    right_load.start()
    for k in range(EARLY):
        send_left(k)
    for hop in (1, 2, 3, 4):
        for sign in (1, -1):
            if sign > 0 or hop < 4:
                ring[sign, hop].wait_recv()
                if hop < (4 if sign > 0 else 3):
                    ring_step(sign, hop + 1)
                spread(-sign * hop if hop < 4 else 4)
    own.wait()
    for k in range(32):
        send_meta(k)

    hands, cores = {}, {}

    def over(q, dx):
        spot = all_ref.at[term(dx), shift(y, ROWS[q], NY)]
        cores[q, dx] = remote(spot, spot, (core_s.at[q, dx % NX], core_r.at[q, dx % NX]), device(dc=1))

    def along(q):
        line = shift(y, ROWS[q], NY)
        for j in range(NZ):
            rows[q - 1, j].wait_recv()
        for i, dx in enumerate((1, -1)):
            spot = all_ref.at[mine, line]
            cols[q, i] = remote(spot, spot, (col_s.at[q, i], col_r.at[q, i]), device(dx=dx))
        over(q, 0)

    def hand_on(q):
        line = shift(y, ROWS[q], NY)
        for i, dx in enumerate((1, -1)):
            if q:
                cols[q, i].wait_recv()
            else:
                for j in range(NZ):
                    cols[0, i, j].wait_recv()
            spot = all_ref.at[term(-dx), line, pl.ds(4 * i, 4)]
            hands[q, i] = remote(spot, spot, (hand_s.at[q, i], hand_r.at[q, i]), device(dx=dx))
            over(q, -dx)
        if q == 0:
            over(q, 0)

    def across(q):
        for i in range(2):
            hands[q, i].wait_recv()
        over(q, 2)

    table = []

    def read_table():
        for copy in metas:
            copy.wait() if copy is metas[0] else copy.wait_recv()
        copy = pltpu.make_async_copy(meta_got, meta_at, own_sem.at[2])
        copy.start()
        table.append(copy)

    ready, loads = set(), {}
    stages = (stage_even, stage_odd)

    def fetch(g):
        for q in (0, 1) if g < 4 else (2, 3):
            if q not in ready:
                ready.add(q)
                for dx in (0, 1, -1, 2):
                    cores[q, dx].wait_recv()
        for i in range(4):
            dz, dy = STEPS[4 * g + i]
            spot = all_ref.at[:, shift(y, -dy, NY), shift(z, -dz, NZ)]
            loads[g, i] = pltpu.make_async_copy(spot, stages[g % 2].at[i], stage_sem.at[g % 2, i])
            loads[g, i].start()

    def group(g):
        if g == 0:
            table[0].wait()
            right_load.wait()
            acc[...] = jnp.zeros_like(acc)
        if (g, 0) not in loads:
            fetch(g)
        for i in range(4):
            loads[g, i].wait()
        if g not in (3, 7):
            fetch(g + 1)
        for k in range(max(4 * g, 1), 4 * g + 4):
            a2a[k].wait_recv()

        def slot(j, carry):
            i, r = j // 2, lax.rem(j, 2)
            code = meta_at[4 * g + i, 0, r]
            live, owner, source = lax.rem(code, 2), lax.rem(code // 2, 4), lax.rem(code // 8, 4)
            left = recv[4 * g + i, r]
            span = pl.ds(pl.multiple_of(j * width, width), width)
            for v in range(2):
                half = jnp.dot(left, stages[g % 2][i, v * 4 + source], preferred_element_type=jnp.float32)
                halves[v * width : (v + 1) * width, span] = half.astype(halves.dtype)
            right = right_ref[code // 32 * 4 + owner]
            for b in range(4):
                keep = (live > 0) & (owner == b)
                picked[b, span, :] = jnp.where(keep, right, jnp.zeros_like(right))
            return carry

        def block(b, carry):
            product = jnp.dot(halves[...], picked[b], preferred_element_type=jnp.float32)
            for v in range(2):
                for t in range(8):
                    at = v * width + t * 32
                    acc[t % 2, t // 2, v, b] += product[at : at + 32]
            return carry

        lax.fori_loop(0, 8, slot, 0, unroll=SLOT_UNROLL)
        lax.fori_loop(0, 4, block, 0, unroll=BLOCK_UNROLL)

    def send_on(first, last):
        paced(max(first, EARLY), last)

    run = dict(send=send_on, table=read_table, along=along, hand=hand_on, cross=across, group=group)
    for kind, *rest in PLAN:
        run[kind](*rest)

    order = (1, -1, 2, 0)
    pairs, sums = [], []
    for i, dx in enumerate(order):
        pairs.append(remote(acc.at[1 - c, shift(x, dx, NX)], pair.at[i], (pair_s.at[i], pair_r.at[i]), device(dc=1)))
    for i, dx in enumerate(order[:3]):
        pairs[i].wait_recv()
        half_sum[i] = (acc[c, shift(x, dx, NX)] + pair[i]).astype(half_sum.dtype)
        sums.append(remote(half_sum.at[i], got.at[i], (sum_s.at[i], sum_r.at[i]), device(dx=dx)))
    pairs[3].wait_recv()
    total = acc[c, x] + pair[3]
    for i in range(3):
        sums[i].wait_recv()
        total += got[i].astype(jnp.float32)
    out_ref[...] = total.astype(out_ref.dtype)

    for group_of in (rows, cols, hands, cores, ring):
        for copy in group_of.values():
            copy.wait_send()
    for copy in [*metas[1:], *a2a[max(32 - WINDOW, 1) :], *pairs, *sums]:
        copy.wait_send()


def shards(wavefunction, left_ops, right_ops, targets):
    group_dev, sector_dev, width, unused = left_ops.shape
    per_dev = group_dev * sector_dev
    sectors = lax.axis_size("sector")
    terms = lax.axis_size("term")
    capacity = 2

    flat_targets = targets.reshape(per_dev)
    dest_dev = flat_targets // sector_dev
    send_slot = dest_dev * capacity + slot_rank(dest_dev)
    lane = jnp.arange(sectors * capacity)
    code = (jnp.arange(per_dev, dtype=jnp.int32) * 4 + flat_targets % sector_dev) * 2 + 1
    code = jnp.sum(jnp.where(send_slot[None, :] == lane[:, None], code[None, :], 0), axis=1)
    code = jnp.pad(code.reshape(sectors, 1, capacity), ((0, 0), (0, 0), (0, 128 - capacity)))

    block = (width, width)
    hbm = pl.BlockSpec(memory_space=pl.ANY)
    vmem = pl.BlockSpec(memory_space=pltpu.VMEM)
    dma = pltpu.SemaphoreType.DMA
    low, wide = jnp.bfloat16, jnp.float32
    piece = (2, sector_dev, width // terms, width)
    out, unused = pl.pallas_call(
        contract_all,
        out_shape=(
            jax.ShapeDtypeStruct(piece, low),
            jax.ShapeDtypeStruct((terms, NY, NZ, *block), low),
        ),
        in_specs=[pl.BlockSpec(memory_space=pltpu.SMEM), vmem, hbm, hbm, hbm],
        out_specs=(vmem, hbm),
        scratch_shapes=[
            pltpu.VMEM((per_dev, *block), low),
            pltpu.VMEM((per_dev, *block), low),
            pltpu.VMEM((sectors, capacity, *block), low),
            pltpu.VMEM((sectors, capacity, *block), low),
            pltpu.VMEM((sectors, 1, 128), jnp.int32),
            pltpu.SMEM((sectors, 1, 128), jnp.int32),
            pltpu.VMEM((4, terms, *block), low),
            pltpu.VMEM((4, terms, *block), low),
            pltpu.VMEM((2 * width, 8 * width), low),
            pltpu.VMEM((4, 8 * width, width), low),
            pltpu.VMEM((2, NX, *piece), wide),
            pltpu.VMEM((NX, *piece), wide),
            pltpu.VMEM((3, *piece), low),
            pltpu.VMEM((3, *piece), low),
            dma((5,)), dma((2, 4)),
            dma((32,)), dma((32,)), dma((32,)), dma((32,)), dma((8,)), dma((8,)), dma((3, 8)), dma((3, 8)), dma((2, 8)), dma((2, 8)),
            dma((4, 2)), dma((4, 2)), dma((4, 2)), dma((4, 2)), dma((4, 4)), dma((4, 4)),
            dma((4,)), dma((4,)), dma((3,)), dma((3,)),
        ],
        compiler_params=pltpu.CompilerParams(
            collective_id=0, has_side_effects=True, vmem_limit_bytes=56 << 20
        ),
    )(
        code, code, left_ops.reshape(per_dev, *block), right_ops.reshape(per_dev, *block),
        wavefunction.reshape(2 * sector_dev, *block),
    )
    return out


def solution(mesh):
    in_specs = (
        P(None, "sector", None, None),
        P("term", "sector", None, None),
        P("term", "sector", None, None),
        P("term", "sector"),
    )
    out_specs = P(None, "sector", "term", None)
    return jax.shard_map(shards, mesh=mesh, in_specs=in_specs, out_specs=out_specs, check_vma=False)
```

```python
import jax
import jax.numpy as jnp
from jax import lax
from jax.experimental import pallas as pl
from jax.experimental.pallas import tpu as pltpu
from jax.sharding import PartitionSpec as P

MESH = pl.DeviceIdType.MESH
NZ, NY, NX = 8, 4, 4
STEPS = [(dz, dy) for pair in ((0, 2), (-1, 1)) for dz in (0, 4, 3, -3, 2, -2, 1, -1) for dy in pair]
ROWS = (0, 2, 1, -1)
NEAR = (0, 1, -1, 2, -2, 3, -3, 4)
WINDOW = 16
EARLY = 4
SLOT_UNROLL = 4
BLOCK_UNROLL = 2
PLAN = [
    ("send", 0, 8), ("along", 1), ("table",), ("send", 8, 12), ("hand", 0), ("along", 2), ("send", 12, 16),
    ("cross", 0), ("hand", 1), ("along", 3), ("send", 16, 20), ("cross", 1), ("hand", 2), ("send", 20, 24),
    ("group", 0), ("group", 1), ("cross", 2), ("hand", 3), ("send", 24, 28), ("group", 2), ("cross", 3),
    ("group", 3), ("send", 28, 32), ("group", 4), ("group", 5), ("group", 6), ("group", 7),
]


def slot_rank(dest_row):
    count = dest_row.shape[0]
    same = dest_row[:, None] == dest_row[None, :]
    lower = jnp.arange(count)[None, :] < jnp.arange(count)[:, None]
    return jnp.sum((same & lower).astype(jnp.int32), axis=1)


def place():
    sector, term = lax.axis_index("sector"), lax.axis_index("term")
    return sector // NY, lax.rem(sector, NY), term // 2, lax.rem(term, 2)


def shift(index, by, size):
    return lax.rem(index + by + size, size)


def contract_all(code_ref, meta_ref, left_hbm, right_hbm, wave_ref, out_ref, all_ref, left_ref, right_ref, send, recv, meta_got, meta_at, stage_even, stage_odd, halves,
                 picked, acc, pair, half_sum, got, own_sem, stage_sem, a2a_s, a2a_r, meta_s, meta_r, ring_s, ring_r,
                 row_s, row_r, near_s, near_r, col_s, col_r, hand_s, hand_r, core_s, core_r, pair_s, pair_r, sum_s, sum_r):
    z, y, x, c = place()
    width = left_ref.shape[-1]
    left_load = pltpu.make_async_copy(left_hbm, left_ref, own_sem.at[3])
    left_load.start()
    right_load = pltpu.make_async_copy(right_hbm, right_ref, own_sem.at[4])

    def device(dz=0, dy=0, dx=0, dc=0):
        return (shift(z, dz, NZ) * NY + shift(y, dy, NY), shift(x, dx, NX) * 2 + lax.rem(c + dc, 2))

    def term(dx):
        return shift(x, dx, NX) * 2 + c

    barrier = pltpu.get_barrier_semaphore()
    partners = [device(dz, dy) for dz, dy in STEPS[1:]] + [device(dx=dx) for dx in (1, -1, 2)] + [device(dc=1)]
    for partner in partners:
        pl.semaphore_signal(barrier, inc=1, device_id=partner, device_id_type=MESH)

    def owner_of(k):
        dz, dy = STEPS[k]
        return shift(z, dz, NZ) * NY + shift(y, dy, NY)

    def pack(k):
        buf = recv if k == 0 else send
        for r in range(2):
            buf[k, r] = left_ref[code_ref[owner_of(k), 0, r] // 8]

    left_load.wait()
    for k in range(EARLY):
        pack(k)
    pl.semaphore_wait(barrier, len(partners))

    def remote(src, dst, sems, where):
        copy = pltpu.make_async_remote_copy(src, dst, *sems, device_id=where, device_id_type=MESH)
        copy.start()
        return copy

    mine = x * 2 + c
    own = pltpu.make_async_copy(wave_ref.at[mine], all_ref.at[mine, y, z], own_sem.at[0])
    own.start()

    ring, rows, cols = {}, {}, {}

    def ring_step(sign, hop):
        k = hop - 1 + (4 if sign < 0 else 0)
        spot = all_ref.at[mine, y, shift(z, -sign * (hop - 1), NZ)]
        src = wave_ref.at[mine] if hop == 1 else spot
        ring[sign, hop] = remote(src, spot, (ring_s.at[k], ring_r.at[k]), device(dz=sign))

    def spread(dz):
        spot = all_ref.at[mine, y, shift(z, dz, NZ)]
        src = spot if dz else wave_ref.at[mine]
        j = NEAR.index(dz)
        for i, dx in enumerate((1, -1)):
            cols[0, i, j] = remote(src, spot, (near_s.at[i, j], near_r.at[i, j]), device(dx=dx))
        for i, dy in enumerate(ROWS[1:]):
            rows[i, j] = remote(src, spot, (row_s.at[i, j], row_r.at[i, j]), device(dy=-dy))

    a2a = []
    metas = []

    def send_meta(k):
        src, dst = meta_ref.at[owner_of(k)], meta_got.at[k]
        if k == 0:
            copy = pltpu.make_async_copy(src, dst, own_sem.at[1])
            copy.start()
        else:
            copy = remote(src, dst, (meta_s.at[k], meta_r.at[k]), device(*STEPS[k]))
        metas.append(copy)

    def send_left(k):
        if k >= EARLY:
            pack(k)
        a2a.append(k and remote(send.at[k], recv.at[k], (a2a_s.at[k], a2a_r.at[k]), device(*STEPS[k])))

    def paced(first, last):
        for k in range(first, last):
            if k > WINDOW:
                a2a[k - WINDOW].wait_send()
            send_left(k)

    ring_step(1, 1)
    ring_step(-1, 1)
    spread(0)
    right_load.start()
    for k in range(EARLY):
        send_left(k)
    for hop in (1, 2, 3, 4):
        for sign in (1, -1):
            if sign > 0 or hop < 4:
                ring[sign, hop].wait_recv()
                if hop < (4 if sign > 0 else 3):
                    ring_step(sign, hop + 1)
                spread(-sign * hop if hop < 4 else 4)
    own.wait()
    for k in range(32):
        send_meta(k)

    hands, cores = {}, {}

    def over(q, dx):
        spot = all_ref.at[term(dx), shift(y, ROWS[q], NY)]
        cores[q, dx] = remote(spot, spot, (core_s.at[q, dx % NX], core_r.at[q, dx % NX]), device(dc=1))

    def along(q):
        line = shift(y, ROWS[q], NY)
        for j in range(NZ):
            rows[q - 1, j].wait_recv()
        for i, dx in enumerate((1, -1)):
            spot = all_ref.at[mine, line]
            cols[q, i] = remote(spot, spot, (col_s.at[q, i], col_r.at[q, i]), device(dx=dx))
        over(q, 0)

    def hand_on(q):
        line = shift(y, ROWS[q], NY)
        for i, dx in enumerate((1, -1)):
            if q:
                cols[q, i].wait_recv()
            else:
                for j in range(NZ):
                    cols[0, i, j].wait_recv()
            spot = all_ref.at[term(-dx), line, pl.ds(4 * i, 4)]
            hands[q, i] = remote(spot, spot, (hand_s.at[q, i], hand_r.at[q, i]), device(dx=dx))
            over(q, -dx)
        if q == 0:
            over(q, 0)

    def across(q):
        for i in range(2):
            hands[q, i].wait_recv()
        over(q, 2)

    table = []

    def read_table():
        for copy in metas:
            copy.wait() if copy is metas[0] else copy.wait_recv()
        copy = pltpu.make_async_copy(meta_got, meta_at, own_sem.at[2])
        copy.start()
        table.append(copy)

    ready, loads = set(), {}
    stages = (stage_even, stage_odd)

    def fetch(g):
        for q in (0, 1) if g < 4 else (2, 3):
            if q not in ready:
                ready.add(q)
                for dx in (0, 1, -1, 2):
                    cores[q, dx].wait_recv()
        for i in range(4):
            dz, dy = STEPS[4 * g + i]
            spot = all_ref.at[:, shift(y, -dy, NY), shift(z, -dz, NZ)]
            loads[g, i] = pltpu.make_async_copy(spot, stages[g % 2].at[i], stage_sem.at[g % 2, i])
            loads[g, i].start()

    def group(g):
        if g == 0:
            table[0].wait()
            right_load.wait()
            acc[...] = jnp.zeros_like(acc)
        if (g, 0) not in loads:
            fetch(g)
        for i in range(4):
            loads[g, i].wait()
        if g not in (3, 7):
            fetch(g + 1)
        for k in range(max(4 * g, 1), 4 * g + 4):
            a2a[k].wait_recv()

        def slot(j, carry):
            i, r = j // 2, lax.rem(j, 2)
            code = meta_at[4 * g + i, 0, r]
            live, owner, source = lax.rem(code, 2), lax.rem(code // 2, 4), lax.rem(code // 8, 4)
            left = recv[4 * g + i, r]
            span = pl.ds(pl.multiple_of(j * width, width), width)
            for v in range(2):
                half = jnp.dot(left, stages[g % 2][i, v * 4 + source], preferred_element_type=jnp.float32)
                halves[v * width : (v + 1) * width, span] = half.astype(halves.dtype)
            right = right_ref[code // 32 * 4 + owner]
            for b in range(4):
                keep = (live > 0) & (owner == b)
                picked[b, span, :] = jnp.where(keep, right, jnp.zeros_like(right))
            return carry

        def block(b, carry):
            product = jnp.dot(halves[...], picked[b], preferred_element_type=jnp.float32)
            for v in range(2):
                for t in range(8):
                    at = v * width + t * 32
                    acc[t % 2, t // 2, v, b] += product[at : at + 32]
            return carry

        lax.fori_loop(0, 8, slot, 0, unroll=SLOT_UNROLL)
        if g < 7:
            lax.fori_loop(0, 4, block, 0, unroll=BLOCK_UNROLL)
            return
        for half in range(2):
            lax.fori_loop(2 * half, 2 * half + 2, block, 0, unroll=BLOCK_UNROLL)
            send_pairs(half)

    order = (1, -1, 2, 0)
    pairs, sums = {}, {}

    def send_pairs(half):
        part = pl.ds(2 * half, 2)
        for i, dx in enumerate(order):
            src, dst = acc.at[1 - c, shift(x, dx, NX), :, part], pair.at[i, :, part]
            pairs[i, half] = remote(src, dst, (pair_s.at[i, half], pair_r.at[i, half]), device(dc=1))

    def send_on(first, last):
        paced(max(first, EARLY), last)

    run = dict(send=send_on, table=read_table, along=along, hand=hand_on, cross=across, group=group)
    for kind, *rest in PLAN:
        run[kind](*rest)

    for half in range(2):
        part = slice(2 * half, 2 * half + 2)
        for i, dx in enumerate(order[:3]):
            pairs[i, half].wait_recv()
            both = acc[c, shift(x, dx, NX), :, part] + pair[i, :, part]
            half_sum[i, :, part] = both.astype(half_sum.dtype)
            spot = pl.ds(2 * half, 2)
            src, dst = half_sum.at[i, :, spot], got.at[i, :, spot]
            sums[i, half] = remote(src, dst, (sum_s.at[i, half], sum_r.at[i, half]), device(dx=dx))
    for half in range(2):
        part = slice(2 * half, 2 * half + 2)
        pairs[3, half].wait_recv()
        total = acc[c, x, :, part] + pair[3, :, part]
        for i in range(3):
            sums[i, half].wait_recv()
            total += got[i, :, part].astype(jnp.float32)
        out_ref[:, part] = total.astype(out_ref.dtype)

    for group_of in (rows, cols, hands, cores, ring, pairs, sums):
        for copy in group_of.values():
            copy.wait_send()
    for copy in [*metas[1:], *a2a[max(32 - WINDOW, 1) :]]:
        copy.wait_send()


def shards(wavefunction, left_ops, right_ops, targets):
    group_dev, sector_dev, width, unused = left_ops.shape
    per_dev = group_dev * sector_dev
    sectors = lax.axis_size("sector")
    terms = lax.axis_size("term")
    capacity = 2

    flat_targets = targets.reshape(per_dev)
    dest_dev = flat_targets // sector_dev
    send_slot = dest_dev * capacity + slot_rank(dest_dev)
    lane = jnp.arange(sectors * capacity)
    code = (jnp.arange(per_dev, dtype=jnp.int32) * 4 + flat_targets % sector_dev) * 2 + 1
    code = jnp.sum(jnp.where(send_slot[None, :] == lane[:, None], code[None, :], 0), axis=1)
    code = jnp.pad(code.reshape(sectors, 1, capacity), ((0, 0), (0, 0), (0, 128 - capacity)))

    block = (width, width)
    hbm = pl.BlockSpec(memory_space=pl.ANY)
    vmem = pl.BlockSpec(memory_space=pltpu.VMEM)
    dma = pltpu.SemaphoreType.DMA
    low, wide = jnp.bfloat16, jnp.float32
    piece = (2, sector_dev, width // terms, width)
    out, unused = pl.pallas_call(
        contract_all,
        out_shape=(
            jax.ShapeDtypeStruct(piece, low),
            jax.ShapeDtypeStruct((terms, NY, NZ, *block), low),
        ),
        in_specs=[pl.BlockSpec(memory_space=pltpu.SMEM), vmem, hbm, hbm, hbm],
        out_specs=(vmem, hbm),
        scratch_shapes=[
            pltpu.VMEM((per_dev, *block), low),
            pltpu.VMEM((per_dev, *block), low),
            pltpu.VMEM((sectors, capacity, *block), low),
            pltpu.VMEM((sectors, capacity, *block), low),
            pltpu.VMEM((sectors, 1, 128), jnp.int32),
            pltpu.SMEM((sectors, 1, 128), jnp.int32),
            pltpu.VMEM((4, terms, *block), low),
            pltpu.VMEM((4, terms, *block), low),
            pltpu.VMEM((2 * width, 8 * width), low),
            pltpu.VMEM((4, 8 * width, width), low),
            pltpu.VMEM((2, NX, *piece), wide),
            pltpu.VMEM((NX, *piece), wide),
            pltpu.VMEM((3, *piece), low),
            pltpu.VMEM((3, *piece), low),
            dma((5,)), dma((2, 4)),
            dma((32,)), dma((32,)), dma((32,)), dma((32,)), dma((8,)), dma((8,)), dma((3, 8)), dma((3, 8)), dma((2, 8)), dma((2, 8)),
            dma((4, 2)), dma((4, 2)), dma((4, 2)), dma((4, 2)), dma((4, 4)), dma((4, 4)),
            dma((4, 2)), dma((4, 2)), dma((3, 2)), dma((3, 2)),
        ],
        compiler_params=pltpu.CompilerParams(
            collective_id=0, has_side_effects=True, vmem_limit_bytes=56 << 20
        ),
    )(
        code, code, left_ops.reshape(per_dev, *block), right_ops.reshape(per_dev, *block),
        wavefunction.reshape(2 * sector_dev, *block),
    )
    return out


def solution(mesh):
    in_specs = (
        P(None, "sector", None, None),
        P("term", "sector", None, None),
        P("term", "sector", None, None),
        P("term", "sector"),
    )
    out_specs = P(None, "sector", "term", None)
    return jax.shard_map(shards, mesh=mesh, in_specs=in_specs, out_specs=out_specs, check_vma=False)
```
